32 devices in a mesh: parts: 2 (over x), seq: 16 (over z, y, core).
Axes of the slice: x: 2, y: 2, z: 4, core: 2. Of those that a mesh axis runs over, the one named last changes fastest.
Arguments:
- control: bfloat16 [256, 3072], P(('parts', 'seq')), parts along dimension 0, may hold values from -6 to 6
- mask_ids: int32 [256], P(('parts', 'seq')), parts along dimension 0, may hold values from 0 to 2
- owner: int32 [256], P('parts'), parts along dimension 0, may hold values from 0 to 127, each once
- mask_table: bfloat16 [3, 3072], replicated, may hold values from -6 to 6
- res_weight: bfloat16 [3072, 3072], P(None, 'seq'), may hold values from -0.109375 to 0.109375
- base: bfloat16 [256, 3072], P(('parts', 'seq')), parts along dimension 0, may hold values from -6 to 6
- modulation: float32 [2, 3072], replicated, may hold values from -0.5 to 0.5
- q_weight: bfloat16 [3072, 1536], P(None, 'seq'), may hold values from -1 to 1
- k_weight: bfloat16 [3072, 1536], P(None, 'seq'), may hold values from -4 to 4
- v_weight: bfloat16 [3072, 1536], P(None, 'seq'), may hold values from -0.109375 to 0.109375
Outputs:
- hidden_out: bfloat16 [256, 3072], P(('parts', 'seq')), parts along dimension 0
- attended: bfloat16 [256, 1536], P(('parts', 'seq')), parts along dimension 0
The draws below stay inside these ranges and needn't reach their ends.
There are 2 independent parts, one for each index of `parts`. The reference program is written for one: setup_inputs(seed, part) draws one part's arguments, and reference() takes and returns one part's arrays. A program takes and returns all parts, laid end to end along the dimension named above; an argument that names none is the same for every part. Nothing has to cross between parts.
Inputs may be any that keep to these rules, and one draw needn't show every extreme that they name: `owner`: each base row is named by exactly one control row.
All inputs are finite; a program needn't handle non-finite values.
Results may differ from the reference program's by a relative error of at most 0.006.
Values may be sent and summed in bfloat16 or wider, within the bound.
A program may use at most 64 MiB of HBM per device.

```python
import math
import jax
import jax.numpy as jnp
from jax import lax

D = 3072
HEADS = 12
HEAD_DIM = 128
MASK_KINDS = 3
TOKENS = 128
HD = 1536


def shared_query(key):
    return jax.random.normal(jax.random.fold_in(key, 11), (D, HEADS * HEAD_DIM), jnp.float32) / math.sqrt(D)


def draw_q_weight(key, part):
    return jnp.clip(shared_query(key), -1.0, 1.0).astype(jnp.bfloat16)


def draw_k_weight(key, part):
    jitter = jax.random.normal(jax.random.fold_in(key, 12), (D, HEADS * HEAD_DIM), jnp.float32) / math.sqrt(D)
    mixed = jitter
    return jnp.clip(mixed, -4.0, 4.0).astype(jnp.bfloat16)


def place_ends(values, stream_key, low, top_value):
    spot = [jax.random.randint(jax.random.fold_in(stream_key, axis), (), 0, length) for axis, length in enumerate(values.shape)]
    widest = values.shape.index(max(values.shape))
    next_to = spot[:widest] + [(spot[widest] + 1) % values.shape[widest]] + spot[widest + 1:]
    return values.at[tuple(spot)].set(low).at[tuple(next_to)].set(top_value)


def block_scale(own_key, extent, shards, least, top_value):
    def one(axis_at, parts):
        heights = jax.random.uniform(jax.random.fold_in(jax.random.fold_in(own_key, 6), axis_at), (parts,), jnp.float32, least / len(shards), top_value / len(shards))
        return jnp.repeat(jnp.exp(heights), extent[axis_at] // parts).reshape((-1,) + (1,) * (len(extent) - axis_at - 1))

    level = one(*shards[0])
    for cut in shards[1:]:
        level = level * one(*cut)
    return level


def bell_draw(stream_key, shape, deviation, reach, pieces=(), held_as=jnp.bfloat16):
    drawn = deviation * jax.random.normal(stream_key, shape, jnp.float32)
    if pieces:
        drawn = drawn * block_scale(stream_key, shape, pieces, -0.22, 0.18)
    return jnp.clip(drawn, -reach, reach).astype(held_as)


def setup_inputs(seed: int = 0, part: int = 0) -> dict:
    streams_of = jax.random.split(jax.random.key(seed), 11)
    part_splits = jax.random.split(jax.random.fold_in(streams_of[10], part), 11)
    return {
        "control": bell_draw(part_splits[0], (TOKENS, D), 1.0, 6.0, ((0, 16),)),
        "mask_ids": place_ends(jax.random.randint(part_splits[1], (TOKENS,), 0, MASK_KINDS), jax.random.fold_in(part_splits[1], 1), 0, MASK_KINDS - 1).astype(jnp.int32),
        "owner": jax.random.permutation(part_splits[2], TOKENS).astype(jnp.int32),
        "mask_table": bell_draw(streams_of[3], (MASK_KINDS, D), 1.0, 6.0),
        "res_weight": bell_draw(streams_of[4], (D, D), D ** -0.5, 0.109375, ((1, 16),)),
        "base": bell_draw(part_splits[5], (TOKENS, D), 1.0, 6.0, ((0, 16),)),
        "modulation": jnp.clip(jax.random.uniform(streams_of[6], (2, D), jnp.float32, -0.5, 0.5), -0.5, 0.5),
        "q_weight": draw_q_weight(jax.random.fold_in(streams_of[10], 71), part),
        "k_weight": draw_k_weight(jax.random.fold_in(streams_of[10], 71), part),
        "v_weight": bell_draw(streams_of[9], (D, HD), D ** -0.5, 0.109375, ((1, 16),)),
    }


def layer_norm(hidden, modulation):
    row_mean = lax.optimization_barrier(jnp.mean(hidden, axis=1, keepdims=True))
    centred = hidden - row_mean
    row_var = lax.optimization_barrier(jnp.mean(centred * centred, axis=1, keepdims=True))
    scaled = centred * lax.rsqrt(row_var + 1e-06)
    return (scaled * (1.0 + modulation[1]) + modulation[0]).astype(jnp.bfloat16)

def one_head(head_args):
    query_head, key_head, value_head = head_args
    scores = jnp.dot(query_head, key_head.T, precision=lax.Precision.HIGHEST, preferred_element_type=jnp.float32) / math.sqrt(HEAD_DIM)
    expo = jnp.exp(scores - lax.optimization_barrier(jnp.max(scores, axis=1, keepdims=True)))
    denom = lax.optimization_barrier(jnp.sum(expo, axis=1, keepdims=True))
    probs = expo.astype(jnp.bfloat16).astype(jnp.float32)
    return jnp.dot(probs, value_head, precision=lax.Precision.HIGHEST, preferred_element_type=jnp.float32) / denom

def split_heads(matrix):
    return matrix.astype(jnp.float32).reshape(TOKENS, HEADS, HEAD_DIM).transpose(1, 0, 2)

def reference(control, mask_ids, owner, mask_table, res_weight, base, modulation, q_weight, k_weight, v_weight):
    selector = (mask_ids[:, None] == jnp.arange(MASK_KINDS, dtype=jnp.int32)[None, :]).astype(jnp.bfloat16)
    condition = (control.astype(jnp.float32) + jnp.dot(selector, mask_table, preferred_element_type=jnp.float32)).astype(jnp.bfloat16)
    residual = jnp.dot(condition, res_weight, preferred_element_type=jnp.float32).astype(jnp.bfloat16)
    inverse = jnp.zeros((TOKENS,), jnp.int32).at[owner].set(jnp.arange(TOKENS, dtype=jnp.int32))
    relayed = jnp.take(residual, inverse, axis=0)
    hidden = base.astype(jnp.float32) + relayed.astype(jnp.float32)
    normed = layer_norm(hidden, modulation)
    queries = jnp.dot(normed, q_weight, preferred_element_type=jnp.float32).astype(jnp.bfloat16)
    key_rows = jnp.dot(normed, k_weight, preferred_element_type=jnp.float32).astype(jnp.bfloat16)
    values = jnp.dot(normed, v_weight, preferred_element_type=jnp.float32).astype(jnp.bfloat16)
    outputs = lax.map(one_head, (split_heads(queries), split_heads(key_rows), split_heads(values)))
    attended = outputs.transpose(1, 0, 2).reshape(TOKENS, HEADS * HEAD_DIM).astype(jnp.bfloat16)
    return (hidden.astype(jnp.bfloat16), attended)
```

```python
import functools
import math

import jax
import jax.numpy as jnp
from jax import lax
from jax.experimental import pallas as pl
from jax.experimental.pallas import tpu as pltpu
from jax.sharding import PartitionSpec as P

HEADS = 12
HEAD_DIM = 128


def layer_norm(hidden, modulation):
    row_mean = jnp.mean(hidden, axis=1, keepdims=True)
    centred = hidden - row_mean
    row_var = jnp.mean(centred * centred, axis=1, keepdims=True)
    scaled = centred * lax.rsqrt(row_var + 1e-06)
    return (scaled * (1.0 + modulation[1]) + modulation[0]).astype(jnp.bfloat16)


def attend_block(carried, segments, query_heads):
    running_max, running_sum, summed = carried
    key_rows, values = segments
    block_rows = key_rows.shape[0]
    key_heads = key_rows.reshape(block_rows, HEADS, HEAD_DIM)
    value_heads = values.reshape(block_rows, HEADS, HEAD_DIM)
    scores = jnp.einsum(
        "thd,khd->thk", query_heads, key_heads, preferred_element_type=jnp.float32
    ) / math.sqrt(HEAD_DIM)
    new_max = jnp.maximum(running_max, jnp.max(scores, axis=2))
    weights = jnp.exp(scores - new_max[:, :, None])
    running_sum = jnp.sum(weights, axis=2)
    summed = jnp.einsum(
        "thk,khd->thd",
        weights.astype(jnp.bfloat16),
        value_heads,
        preferred_element_type=jnp.float32,
    )
    return (new_max, running_sum, summed)


def on_device(
    control, mask_ids, owner, mask_table, res_weight, base, modulation, q_weight, k_weight, v_weight
):
    row_count = base.shape[0]
    selector = (
        mask_ids[:, None] == jnp.arange(mask_table.shape[0], dtype=jnp.int32)[None, :]
    ).astype(jnp.bfloat16)
    condition = (
        control.astype(jnp.float32)
        + jnp.dot(selector, mask_table, preferred_element_type=jnp.float32)
    ).astype(jnp.bfloat16)
    residual = jnp.dot(
        lax.all_gather(condition, "seq", axis=0, tiled=True),
        res_weight,
        preferred_element_type=jnp.float32,
    ).astype(jnp.bfloat16)
    total_rows = owner.shape[0]
    inverse = (
        jnp.zeros((total_rows,), jnp.int32).at[owner].set(jnp.arange(total_rows, dtype=jnp.int32))
    )
    relayed = lax.all_to_all(
        jnp.take(residual, inverse, axis=0), "seq", split_axis=0, concat_axis=1, tiled=True
    )
    hidden = base.astype(jnp.float32) + relayed.astype(jnp.float32)
    normed = layer_norm(hidden, modulation)
    joined = jnp.concatenate([q_weight, k_weight, v_weight], axis=1)
    col_width = q_weight.shape[1]
    columns = jnp.dot(
        lax.all_gather(normed, "seq", axis=0, tiled=True),
        joined,
        preferred_element_type=jnp.float32,
    ).astype(jnp.bfloat16)
    q_cols = columns[:, :col_width]
    k_cols = columns[:, col_width : 2 * col_width]
    v_cols = columns[:, 2 * col_width :]
    initial = (
        jnp.full((row_count, HEADS), -1e30, jnp.float32),
        jnp.zeros((row_count, HEADS), jnp.float32),
        jnp.zeros((row_count, HEADS, HEAD_DIM), jnp.float32),
    )
    queries = lax.all_to_all(q_cols, "seq", split_axis=0, concat_axis=1, tiled=True)
    key_rows, values = (
        lax.all_gather(k_cols, "seq", axis=1, tiled=True),
        lax.all_gather(v_cols, "seq", axis=1, tiled=True),
    )
    query_heads = queries.reshape(row_count, HEADS, HEAD_DIM)
    running_max, running_sum, summed = attend_block(initial, (key_rows, values), query_heads)
    attended = (
        (summed / running_sum[:, :, None]).reshape(row_count, HEADS * HEAD_DIM).astype(jnp.bfloat16)
    )
    return (hidden.astype(jnp.bfloat16), attended)


def remote(src, dst, send_sem, recv_sem, target):
    return pltpu.make_async_remote_copy(
        src_ref=src,
        dst_ref=dst,
        send_sem=send_sem,
        recv_sem=recv_sem,
        device_id={"seq": target},
        device_id_type=pl.DeviceIdType.MESH,
    )


def dot_last(a, b):
    return lax.dot_general(
        a, b, (((1,), (1,)), ((), ())), preferred_element_type=jnp.float32
    )


def one_hot(condition):
    return jnp.where(condition, 1.0, 0.0).astype(jnp.bfloat16)


def fused_kernel(
    seq,
    owner_ref,
    ids_ref,
    table_ref,
    mod_ref,
    control_ref,
    base_ref,
    wres_hbm,
    wq_hbm,
    wk_hbm,
    wv_hbm,
    hid_ref,
    att_ref,
    wres,
    wqkv,
    cond_all,
    base_all,
    hid_all,
    qkv_own,
    qkv_mid,
    part_send,
    part_recv,
    out_send,
    out_recv,
    load_sem,
    wsend_sem,
    wrecv_sem,
    csend_sem,
    crecv_sem,
    bsend_sem,
    brecv_sem,
    hsend_sem,
    hrecv_sem,
    msend_sem,
    orecv_sem,
    mrecv_sem,
    psend_sem,
    precv_sem,
    asend_sem,
    arecv_sem,
):
    me = lax.axis_index("seq")
    core = lax.rem(me, 2)
    chip = lax.div(me, 2)
    row = lax.rem(chip, 2)
    line = lax.div(chip, 2)
    chips = seq // 2
    lines = chips // 2
    sibling = chip * 2 + 1 - core
    rows, width = control_ref.shape
    tokens = rows * seq
    half = tokens // 2
    chip_cols = width // chips
    heads = att_ref.shape[1] // HEAD_DIM

    weights = (wres_hbm, wq_hbm, wk_hbm, wv_hbm)

    def slot(i, which):
        return wres.at[which] if i == 0 else wqkv.at[i - 1, which]

    loads = [
        pltpu.make_async_copy(weights[i], slot(i, core), load_sem.at[i]) for i in range(4)
    ]
    for load in loads:
        load.start()

    barrier = pltpu.get_barrier_semaphore()
    for step in range(1, seq):
        pl.semaphore_signal(
            barrier,
            inc=1,
            device_id={"seq": lax.rem(me + step, seq)},
            device_id_type=pl.DeviceIdType.MESH,
        )

    row_at = lax.broadcasted_iota(jnp.int32, (rows, width), 0)
    kinds = jnp.zeros((rows, width), jnp.int32)
    for r in range(rows):
        kinds = jnp.where(row_at == r, ids_ref[r], kinds)
    picked = jnp.zeros((rows, width), jnp.float32)
    for kind in range(table_ref.shape[0]):
        entry = table_ref[kind : kind + 1, :].astype(jnp.float32)
        picked = jnp.where(kinds == kind, entry, picked)
    cond_all[chip] = (control_ref[...].astype(jnp.float32) + picked).astype(jnp.bfloat16)
    for j in range(chips):
        base_all[me, j] = base_ref[:, j * chip_cols : (j + 1) * chip_cols]

    pl.semaphore_wait(barrier, seq - 1)

    def along(step):
        return lax.rem(line + step, lines) * 2

    def gather_sends(buf, send_sem, recv_sem):
        copies = []
        for step in range(1, lines):
            target = (along(step) + row) * 2 + core
            copies.append(
                remote(buf.at[chip], buf.at[chip], send_sem.at[step], recv_sem.at[chip], target)
            )
        target = (line * 2 + 1 - row) * 2 + core
        copies.insert(
            0, remote(buf.at[chip], buf.at[chip], send_sem.at[0], recv_sem.at[chip], target)
        )
        for copy in copies:
            copy.start()
        return copies

    across = (line * 2 + 1 - row) * 2 + core

    def arrival(buf, send_sem, recv_sem, source):
        remote(buf.at[source], buf.at[source], send_sem.at[0], recv_sem.at[source], across).wait_recv()

    def forward(buf, send_sem, recv_sem, step):
        source = along(lines - step) + row
        arrival(buf, send_sem, recv_sem, source)
        copy = remote(
            buf.at[source], buf.at[source], send_sem.at[lines - 1 + step], recv_sem.at[source], across
        )
        copy.start()
        return source, copy

    cond_copies = gather_sends(cond_all, csend_sem, crecv_sem)
    weight_copies = [
        remote(weights[i], slot(i, core), wsend_sem.at[i], wrecv_sem.at[i], sibling)
        for i in range(4)
    ]
    weight_copies[0].start()

    base_copies = []
    for step in range(1, seq):
        target = lax.rem(me + step, seq)
        copy = remote(
            base_all.at[me, lax.div(target, 2)],
            base_all.at[me, lax.div(target, 2)],
            bsend_sem.at[step],
            brecv_sem.at[me],
            target,
        )
        copy.start()
        base_copies.append(copy)
    for copy in weight_copies[1:]:
        copy.start()

    for step in range(1, lines):
        cond_copies.append(forward(cond_all, csend_sem, crecv_sem, step)[1])

    owned = one_hot(
        lax.broadcasted_iota(jnp.int32, (tokens, tokens), 0) == owner_ref[...]
    )

    def control_row(count, first):
        at = first + lax.broadcasted_iota(jnp.int32, (count, tokens), 0)
        part = at // half
        inner = at % half
        index = (inner // rows) * (2 * rows) + part * rows + inner % rows
        return one_hot(index == lax.broadcasted_iota(jnp.int32, (count, tokens), 1))

    mine = control_row(half, core * half)
    base_of = dot_last(mine, owned).astype(jnp.bfloat16)

    loads[0].wait()
    weight_copies[0].wait_recv()
    arrival(cond_all, csend_sem, crecv_sem, across // 2)
    for step in range(1, lines):
        arrival(cond_all, csend_sem, crecv_sem, along(lines - step) + 1 - row)
    for step in range(1, seq):
        source = lax.rem(me + seq - step, seq)
        remote(
            base_all.at[source, chip],
            base_all.at[source, chip],
            bsend_sem.at[step],
            brecv_sem.at[source],
            sibling,
        ).wait_recv()

    condition = cond_all[...].reshape(half, width)
    residual = jnp.concatenate(
        [jnp.dot(condition, wres[which], preferred_element_type=jnp.float32) for which in range(2)],
        axis=1,
    ).astype(jnp.bfloat16)
    base_cols = jnp.concatenate([base_all[s, chip] for s in range(seq)], axis=0)
    base_rows = jnp.dot(base_of, base_cols, preferred_element_type=jnp.float32)
    hid_all[chip] = (base_rows + residual.astype(jnp.float32)).astype(jnp.bfloat16)

    hid_copies = gather_sends(hid_all, hsend_sem, hrecv_sem)

    for i in range(1, 4):
        loads[i].wait()
        weight_copies[i].wait_recv()

    for step in range(1, lines):
        hid_copies.append(forward(hid_all, hsend_sem, hrecv_sem, step)[1])
    arrival(hid_all, hsend_sem, hrecv_sem, across // 2)
    for step in range(1, lines):
        arrival(hid_all, hsend_sem, hrecv_sem, along(lines - step) + 1 - row)

    total = jnp.zeros((half, 1), jnp.float32)
    for j in range(chips):
        total += jnp.sum(hid_all[j].astype(jnp.float32), axis=1, keepdims=True)
    mean = total / width
    total = jnp.zeros((half, 1), jnp.float32)
    for j in range(chips):
        centred = hid_all[j].astype(jnp.float32) - mean
        total += jnp.sum(centred * centred, axis=1, keepdims=True)
    scale = lax.rsqrt(total / width + 1e-06)

    columns = [[jnp.zeros((half, wqkv.shape[3]), jnp.float32) for _ in range(2)] for _ in range(3)]
    for j in range(chips):
        span = slice(j * chip_cols, (j + 1) * chip_cols)
        block = hid_all[j].astype(jnp.float32)
        normed = (
            (block - mean) * scale * (1.0 + mod_ref[1:2, span]) + mod_ref[0:1, span]
        ).astype(jnp.bfloat16)
        for i in range(3):
            for which in range(2):
                columns[i][which] += jnp.dot(
                    normed, wqkv[i, which, span, :], preferred_element_type=jnp.float32
                )

    pad = 2 * HEAD_DIM - 2 * wqkv.shape[3]
    blank = jnp.zeros((half, pad), jnp.float32)
    for i in range(3):
        first = jnp.concatenate([columns[i][0], columns[i][1], blank], axis=1)
        second = jnp.concatenate([blank, columns[i][0], columns[i][1]], axis=1)
        own = jnp.where(row == 0, first[:, :HEAD_DIM], second[:, HEAD_DIM:])
        middle = jnp.where(row == 0, first[:, HEAD_DIM:], second[:, :HEAD_DIM])
        span = slice(i * HEAD_DIM, (i + 1) * HEAD_DIM)
        qkv_own[core, :, span] = own.astype(jnp.bfloat16)
        qkv_mid[row, core, :, span] = middle.astype(jnp.bfloat16)

    middle_at = line * 4 + 1
    takes_own = core == row
    takes_middle = jnp.logical_and(row == 0, core == 1)
    own_copy = remote(
        qkv_own.at[core], qkv_own.at[core], msend_sem.at[0], orecv_sem, sibling
    )
    mid_copy = remote(
        qkv_mid.at[row, core],
        qkv_mid.at[row, core],
        msend_sem.at[1],
        mrecv_sem.at[row * 2 + core],
        middle_at,
    )

    @pl.when(jnp.logical_not(takes_own))
    def _():
        own_copy.start()

    @pl.when(jnp.logical_not(takes_middle))
    def _():
        mid_copy.start()

    chosen = []
    for first in (me * rows, sibling * rows):
        named = one_hot(
            first + lax.broadcasted_iota(jnp.int32, (rows, tokens), 0) == owner_ref[...]
        )
        chosen.append(named)
    chosen = dot_last(jnp.concatenate(chosen, axis=0), mine).astype(jnp.bfloat16)
    for j in range(chips):
        span = slice(j * chip_cols, (j + 1) * chip_cols)
        piece = jnp.dot(chosen, hid_all[j], preferred_element_type=jnp.float32)
        hid_ref[:, span] = piece[:rows].astype(jnp.bfloat16)
        part_send[:, span] = piece[rows:].astype(jnp.bfloat16)
    part_copy = remote(part_send, part_recv, psend_sem, precv_sem, sibling)
    part_copy.start()

    to_base = dot_last(owned, control_row(tokens, 0)).astype(jnp.bfloat16)

    def attend(queries, keys, values):
        queries = jnp.dot(to_base, queries, preferred_element_type=jnp.float32).astype(jnp.bfloat16)
        scores = dot_last(queries, keys) / math.sqrt(HEAD_DIM)
        expo = jnp.exp(scores - jnp.max(scores, axis=1, keepdims=True))
        denom = jnp.sum(expo, axis=1, keepdims=True)
        summed = jnp.dot(expo.astype(jnp.bfloat16), values, preferred_element_type=jnp.float32)
        out_send[...] = summed / denom

    head = line * 3 + row + core

    @pl.when(takes_own)
    def _():
        remote(
            qkv_own.at[1 - core], qkv_own.at[1 - core], msend_sem.at[0], orecv_sem, sibling
        ).wait_recv()
        joined = jnp.concatenate([qkv_own[0], qkv_own[1]], axis=0)
        attend(*[joined[:, i * HEAD_DIM : (i + 1) * HEAD_DIM] for i in range(3)])

    @pl.when(takes_middle)
    def _():
        for at in ((0, 0), (1, 0), (1, 1)):
            remote(
                qkv_mid.at[at[0], at[1]],
                qkv_mid.at[at[0], at[1]],
                msend_sem.at[1],
                mrecv_sem.at[at[0] * 2 + at[1]],
                sibling,
            ).wait_recv()
        joined = jnp.concatenate(
            [qkv_mid[0, which] + qkv_mid[1, which] for which in range(2)], axis=0
        )
        attend(*[joined[:, i * HEAD_DIM : (i + 1) * HEAD_DIM] for i in range(3)])

    works = jnp.logical_or(takes_own, takes_middle)

    def out_copy(step):
        target = lax.rem(me + step, seq)
        return remote(
            out_send.at[pl.ds(pl.multiple_of(target * rows, rows), rows)],
            out_recv.at[head],
            asend_sem.at[step],
            arecv_sem.at[head],
            target,
        )

    @pl.when(works)
    def _():
        for step in range(1, seq):
            out_copy(step).start()
        out_recv[head] = out_send[pl.ds(pl.multiple_of(me * rows, rows), rows), :]

    part_copy.wait_recv()
    hid_ref[...] = hid_ref[...] + part_recv[...]

    for copy in cond_copies + base_copies + weight_copies + hid_copies:
        copy.wait_send()

    @pl.when(jnp.logical_not(takes_own))
    def _():
        own_copy.wait_send()

    @pl.when(jnp.logical_not(takes_middle))
    def _():
        mid_copy.wait_send()

    part_copy.wait_send()

    for h in range(heads):
        which = h % 3
        source = (h // 3) * 4 + (0, 1, 3)[which]

        @pl.when(source != me)
        def _():
            remote(
                out_recv.at[h], out_recv.at[h], asend_sem.at[0], arecv_sem.at[h], sibling
            ).wait_recv()

        att_ref[:, h * HEAD_DIM : (h + 1) * HEAD_DIM] = out_recv[h].astype(jnp.bfloat16)

    @pl.when(works)
    def _():
        for step in range(1, seq):
            out_copy(step).wait_send()


def on_device_fused(
    seq,
    control, mask_ids, owner, mask_table, res_weight, base, modulation, q_weight, k_weight, v_weight
):
    rows, width = control.shape
    chips = seq // 2
    heads_width = q_weight.shape[1] * seq
    fits = (
        seq % 4 == 0
        and rows == 8
        and width % (chips * HEAD_DIM) == 0
        and q_weight.shape[1] * 8 == 3 * 2 * HEAD_DIM
        and (rows * seq) % HEAD_DIM == 0
        and rows * seq <= 256
    )
    if not fits:
        return on_device(
            control, mask_ids, owner, mask_table, res_weight, base, modulation, q_weight, k_weight, v_weight
        )
    tokens = rows * seq
    half = tokens // 2
    chip_cols = width // chips
    bf16 = jnp.bfloat16
    vmem = pl.BlockSpec(memory_space=pltpu.VMEM)
    hbm = pl.BlockSpec(memory_space=pl.ANY)
    dma = pltpu.SemaphoreType.DMA
    lines = chips // 2
    return pl.pallas_call(
        functools.partial(fused_kernel, seq),
        out_shape=(
            jax.ShapeDtypeStruct((rows, width), bf16),
            jax.ShapeDtypeStruct((rows, heads_width), bf16),
        ),
        in_specs=[vmem, pl.BlockSpec(memory_space=pltpu.SMEM)] + [vmem] * 4 + [hbm] * 4,
        out_specs=(vmem, vmem),
        scratch_shapes=[
            pltpu.VMEM((2, width, res_weight.shape[1]), bf16),
            pltpu.VMEM((3, 2, width, q_weight.shape[1]), bf16),
            pltpu.VMEM((chips, rows, width), bf16),
            pltpu.VMEM((seq, chips, rows, chip_cols), bf16),
            pltpu.VMEM((chips, half, chip_cols), bf16),
            pltpu.VMEM((2, half, 3 * HEAD_DIM), bf16),
            pltpu.VMEM((2, 2, half, 3 * HEAD_DIM), bf16),
            pltpu.VMEM((rows, width), bf16),
            pltpu.VMEM((rows, width), bf16),
            pltpu.VMEM((tokens, HEAD_DIM), jnp.float32),
            pltpu.VMEM((heads_width // HEAD_DIM, rows, HEAD_DIM), jnp.float32),
            dma((4,)),
            dma((4,)),
            dma((4,)),
            dma((2 * lines,)),
            dma((chips,)),
            dma((seq,)),
            dma((seq,)),
            dma((2 * lines,)),
            dma((chips,)),
            dma((2,)),
            dma(()),
            dma((4,)),
            dma(()),
            dma(()),
            dma((seq,)),
            dma((heads_width // HEAD_DIM,)),
        ],
        compiler_params=pltpu.CompilerParams(
            collective_id=0, has_side_effects=True, vmem_limit_bytes=40 * 1024 * 1024
        ),
    )(
        owner.reshape(1, tokens),
        mask_ids,
        mask_table,
        modulation,
        control,
        base,
        res_weight,
        q_weight,
        k_weight,
        v_weight,
    )


def solution(mesh):
    in_specs = (
        P(("parts", "seq"), None),
        P(("parts", "seq")),
        P("parts"),
        P(),
        P(None, "seq"),
        P(("parts", "seq"), None),
        P(),
        P(None, "seq"),
        P(None, "seq"),
        P(None, "seq"),
    )
    out_specs = (P(("parts", "seq"), None), P(("parts", "seq"), None))
    body = functools.partial(on_device_fused, mesh.shape["seq"])
    return jax.shard_map(
        body, mesh=mesh, in_specs=in_specs, out_specs=out_specs, check_vma=False
    )
```

```python
import functools
import math

import jax
import jax.numpy as jnp
from jax import lax
from jax.experimental import pallas as pl
from jax.experimental.pallas import tpu as pltpu
from jax.sharding import PartitionSpec as P

HEADS = 12
HEAD_DIM = 128


def layer_norm(hidden, modulation):
    row_mean = jnp.mean(hidden, axis=1, keepdims=True)
    centred = hidden - row_mean
    row_var = jnp.mean(centred * centred, axis=1, keepdims=True)
    scaled = centred * lax.rsqrt(row_var + 1e-06)
    return (scaled * (1.0 + modulation[1]) + modulation[0]).astype(jnp.bfloat16)


def attend_block(carried, segments, query_heads):
    running_max, running_sum, summed = carried
    key_rows, values = segments
    block_rows = key_rows.shape[0]
    key_heads = key_rows.reshape(block_rows, HEADS, HEAD_DIM)
    value_heads = values.reshape(block_rows, HEADS, HEAD_DIM)
    scores = jnp.einsum(
        "thd,khd->thk", query_heads, key_heads, preferred_element_type=jnp.float32
    ) / math.sqrt(HEAD_DIM)
    new_max = jnp.maximum(running_max, jnp.max(scores, axis=2))
    weights = jnp.exp(scores - new_max[:, :, None])
    running_sum = jnp.sum(weights, axis=2)
    summed = jnp.einsum(
        "thk,khd->thd",
        weights.astype(jnp.bfloat16),
        value_heads,
        preferred_element_type=jnp.float32,
    )
    return (new_max, running_sum, summed)


def on_device(
    control, mask_ids, owner, mask_table, res_weight, base, modulation, q_weight, k_weight, v_weight
):
    row_count = base.shape[0]
    selector = (
        mask_ids[:, None] == jnp.arange(mask_table.shape[0], dtype=jnp.int32)[None, :]
    ).astype(jnp.bfloat16)
    condition = (
        control.astype(jnp.float32)
        + jnp.dot(selector, mask_table, preferred_element_type=jnp.float32)
    ).astype(jnp.bfloat16)
    residual = jnp.dot(
        lax.all_gather(condition, "seq", axis=0, tiled=True),
        res_weight,
        preferred_element_type=jnp.float32,
    ).astype(jnp.bfloat16)
    total_rows = owner.shape[0]
    inverse = (
        jnp.zeros((total_rows,), jnp.int32).at[owner].set(jnp.arange(total_rows, dtype=jnp.int32))
    )
    relayed = lax.all_to_all(
        jnp.take(residual, inverse, axis=0), "seq", split_axis=0, concat_axis=1, tiled=True
    )
    hidden = base.astype(jnp.float32) + relayed.astype(jnp.float32)
    normed = layer_norm(hidden, modulation)
    joined = jnp.concatenate([q_weight, k_weight, v_weight], axis=1)
    col_width = q_weight.shape[1]
    columns = jnp.dot(
        lax.all_gather(normed, "seq", axis=0, tiled=True),
        joined,
        preferred_element_type=jnp.float32,
    ).astype(jnp.bfloat16)
    q_cols = columns[:, :col_width]
    k_cols = columns[:, col_width : 2 * col_width]
    v_cols = columns[:, 2 * col_width :]
    initial = (
        jnp.full((row_count, HEADS), -1e30, jnp.float32),
        jnp.zeros((row_count, HEADS), jnp.float32),
        jnp.zeros((row_count, HEADS, HEAD_DIM), jnp.float32),
    )
    queries = lax.all_to_all(q_cols, "seq", split_axis=0, concat_axis=1, tiled=True)
    key_rows, values = (
        lax.all_gather(k_cols, "seq", axis=1, tiled=True),
        lax.all_gather(v_cols, "seq", axis=1, tiled=True),
    )
    query_heads = queries.reshape(row_count, HEADS, HEAD_DIM)
    running_max, running_sum, summed = attend_block(initial, (key_rows, values), query_heads)
    attended = (
        (summed / running_sum[:, :, None]).reshape(row_count, HEADS * HEAD_DIM).astype(jnp.bfloat16)
    )
    return (hidden.astype(jnp.bfloat16), attended)


def remote(src, dst, send_sem, recv_sem, target):
    return pltpu.make_async_remote_copy(
        src_ref=src,
        dst_ref=dst,
        send_sem=send_sem,
        recv_sem=recv_sem,
        device_id={"seq": target},
        device_id_type=pl.DeviceIdType.MESH,
    )


def dot_last(a, b):
    return lax.dot_general(
        a, b, (((1,), (1,)), ((), ())), preferred_element_type=jnp.float32
    )


def one_hot(condition):
    return jnp.where(condition, 1.0, 0.0).astype(jnp.bfloat16)


def fused_kernel(
    seq,
    owner_ref,
    ids_ref,
    table_hbm,
    mod_hbm,
    control_hbm,
    base_hbm,
    wres_hbm,
    wq_hbm,
    wk_hbm,
    wv_hbm,
    hid_ref,
    att_ref,
    table_ref,
    mod_ref,
    control_ref,
    base_ref,
    wres,
    wqkv,
    cond_all,
    base_all,
    hid_all,
    qkv_own,
    qkv_mid,
    part_send,
    part_recv,
    out_send,
    out_recv,
    load_sem,
    wsend_sem,
    wrecv_sem,
    csend_sem,
    crecv_sem,
    bsend_sem,
    brecv_sem,
    hsend_sem,
    hrecv_sem,
    msend_sem,
    orecv_sem,
    mrecv_sem,
    psend_sem,
    precv_sem,
    asend_sem,
    arecv_sem,
):
    me = lax.axis_index("seq")
    core = lax.rem(me, 2)
    chip = lax.div(me, 2)
    row = lax.rem(chip, 2)
    line = lax.div(chip, 2)
    chips = seq // 2
    lines = chips // 2
    sibling = chip * 2 + 1 - core
    rows, width = control_hbm.shape
    tokens = rows * seq
    half = tokens // 2
    chip_cols = width // chips
    heads = att_ref.shape[1] // HEAD_DIM

    weights = (wres_hbm, wq_hbm, wk_hbm, wv_hbm)

    def slot(i, which):
        return wres.at[which] if i == 0 else wqkv.at[i - 1, which]

    loads = [
        pltpu.make_async_copy(weights[i], slot(i, core), load_sem.at[i]) for i in range(4)
    ]
    inputs = (
        (control_hbm, control_ref),
        (table_hbm, table_ref),
        (base_hbm, base_ref),
        (mod_hbm, mod_ref),
    )
    for i, (source, kept) in enumerate(inputs):
        loads.append(pltpu.make_async_copy(source, kept, load_sem.at[4 + i]))
    for load in loads[4:] + loads[:4]:
        load.start()

    barrier = pltpu.get_barrier_semaphore()
    for step in range(1, seq):
        pl.semaphore_signal(
            barrier,
            inc=1,
            device_id={"seq": lax.rem(me + step, seq)},
            device_id_type=pl.DeviceIdType.MESH,
        )

    for load in loads[4:]:
        load.wait()
    row_at = lax.broadcasted_iota(jnp.int32, (rows, width), 0)
    kinds = jnp.zeros((rows, width), jnp.int32)
    for r in range(rows):
        kinds = jnp.where(row_at == r, ids_ref[r], kinds)
    picked = jnp.zeros((rows, width), jnp.float32)
    for kind in range(table_ref.shape[0]):
        entry = table_ref[kind : kind + 1, :].astype(jnp.float32)
        picked = jnp.where(kinds == kind, entry, picked)
    cond_all[chip] = (control_ref[...].astype(jnp.float32) + picked).astype(jnp.bfloat16)
    for j in range(chips):
        base_all[me, j] = base_ref[:, j * chip_cols : (j + 1) * chip_cols]

    pl.semaphore_wait(barrier, seq - 1)

    def along(step):
        return lax.rem(line + step, lines) * 2

    def gather_sends(buf, send_sem, recv_sem):
        copies = []
        for step in range(1, lines):
            target = (along(step) + row) * 2 + core
            copies.append(
                remote(buf.at[chip], buf.at[chip], send_sem.at[step], recv_sem.at[chip], target)
            )
        target = (line * 2 + 1 - row) * 2 + core
        copies.insert(
            0, remote(buf.at[chip], buf.at[chip], send_sem.at[0], recv_sem.at[chip], target)
        )
        for copy in copies:
            copy.start()
        return copies

    across = (line * 2 + 1 - row) * 2 + core

    def arrival(buf, send_sem, recv_sem, source):
        remote(buf.at[source], buf.at[source], send_sem.at[0], recv_sem.at[source], across).wait_recv()

    def forward(buf, send_sem, recv_sem, step):
        source = along(lines - step) + row
        arrival(buf, send_sem, recv_sem, source)
        copy = remote(
            buf.at[source], buf.at[source], send_sem.at[lines - 1 + step], recv_sem.at[source], across
        )
        copy.start()
        return source, copy

    cond_copies = gather_sends(cond_all, csend_sem, crecv_sem)
    weight_copies = [
        remote(weights[i], slot(i, core), wsend_sem.at[i], wrecv_sem.at[i], sibling)
        for i in range(4)
    ]
    weight_copies[0].start()

    base_copies = []
    for step in range(1, seq):
        target = lax.rem(me + step, seq)
        copy = remote(
            base_all.at[me, lax.div(target, 2)],
            base_all.at[me, lax.div(target, 2)],
            bsend_sem.at[step],
            brecv_sem.at[me],
            target,
        )
        copy.start()
        base_copies.append(copy)
    for copy in weight_copies[1:]:
        copy.start()

    for step in range(1, lines):
        cond_copies.append(forward(cond_all, csend_sem, crecv_sem, step)[1])

    owned = one_hot(
        lax.broadcasted_iota(jnp.int32, (tokens, tokens), 0) == owner_ref[...]
    )

    def control_row(count, first):
        at = first + lax.broadcasted_iota(jnp.int32, (count, tokens), 0)
        part = jnp.where(at >= half, 1, 0)
        inner = at - part * half
        shift = rows.bit_length() - 1
        index = (
            lax.shift_left(lax.shift_right_logical(inner, shift), shift + 1)
            + part * rows
            + lax.bitwise_and(inner, rows - 1)
        )
        return one_hot(index == lax.broadcasted_iota(jnp.int32, (count, tokens), 1))

    mine = control_row(half, core * half)
    base_of = dot_last(mine, owned).astype(jnp.bfloat16)

    loads[0].wait()
    weight_copies[0].wait_recv()
    arrival(cond_all, csend_sem, crecv_sem, across // 2)
    for step in range(1, lines):
        arrival(cond_all, csend_sem, crecv_sem, along(lines - step) + 1 - row)
    for step in range(1, seq):
        source = lax.rem(me + seq - step, seq)
        remote(
            base_all.at[source, chip],
            base_all.at[source, chip],
            bsend_sem.at[step],
            brecv_sem.at[source],
            sibling,
        ).wait_recv()

    condition = cond_all[...].reshape(half, width)
    residual = dot_last(condition, wres[...].reshape(chip_cols, width)).astype(jnp.bfloat16)
    base_cols = jnp.concatenate([base_all[s, chip] for s in range(seq)], axis=0)
    base_rows = jnp.dot(base_of, base_cols, preferred_element_type=jnp.float32)
    hid_all[chip] = (base_rows + residual.astype(jnp.float32)).astype(jnp.bfloat16)

    hid_copies = gather_sends(hid_all, hsend_sem, hrecv_sem)

    for i in range(1, 4):
        loads[i].wait()
        weight_copies[i].wait_recv()

    for step in range(1, lines):
        hid_copies.append(forward(hid_all, hsend_sem, hrecv_sem, step)[1])
    arrival(hid_all, hsend_sem, hrecv_sem, across // 2)
    for step in range(1, lines):
        arrival(hid_all, hsend_sem, hrecv_sem, along(lines - step) + 1 - row)

    total = jnp.zeros((half, 1), jnp.float32)
    for j in range(chips):
        total += jnp.sum(hid_all[j].astype(jnp.float32), axis=1, keepdims=True)
    mean = total / width
    total = jnp.zeros((half, 1), jnp.float32)
    for j in range(chips):
        centred = hid_all[j].astype(jnp.float32) - mean
        total += jnp.sum(centred * centred, axis=1, keepdims=True)
    scale = lax.rsqrt(total / width + 1e-06)

    local = 2 * wqkv.shape[2]
    columns = [jnp.zeros((half, local), jnp.float32) for _ in range(3)]
    for j in range(chips):
        span = slice(j * chip_cols, (j + 1) * chip_cols)
        block = hid_all[j].astype(jnp.float32)
        normed = (
            (block - mean) * scale * (1.0 + mod_ref[1:2, span]) + mod_ref[0:1, span]
        ).astype(jnp.bfloat16)
        for i in range(3):
            columns[i] += dot_last(normed, wqkv[i, :, :, span].reshape(local, chip_cols))

    blank = jnp.zeros((half, 2 * HEAD_DIM - local), jnp.float32)
    for i in range(3):
        first = jnp.concatenate([columns[i], blank], axis=1)
        second = jnp.concatenate([blank, columns[i]], axis=1)
        own = jnp.where(row == 0, first[:, :HEAD_DIM], second[:, HEAD_DIM:])
        middle = jnp.where(row == 0, first[:, HEAD_DIM:], second[:, :HEAD_DIM])
        span = slice(i * HEAD_DIM, (i + 1) * HEAD_DIM)
        qkv_own[core, :, span] = own.astype(jnp.bfloat16)
        qkv_mid[row, core, :, span] = middle.astype(jnp.bfloat16)

    middle_at = line * 4 + 1
    takes_own = core == row
    takes_middle = jnp.logical_and(row == 0, core == 1)
    own_copy = remote(
        qkv_own.at[core], qkv_own.at[core], msend_sem.at[0], orecv_sem, sibling
    )
    mid_copy = remote(
        qkv_mid.at[row, core],
        qkv_mid.at[row, core],
        msend_sem.at[1],
        mrecv_sem.at[row * 2 + core],
        middle_at,
    )

    @pl.when(jnp.logical_not(takes_own))
    def _():
        own_copy.start()

    @pl.when(jnp.logical_not(takes_middle))
    def _():
        mid_copy.start()

    chosen = []
    for first in (me * rows, sibling * rows):
        named = one_hot(
            first + lax.broadcasted_iota(jnp.int32, (rows, tokens), 0) == owner_ref[...]
        )
        chosen.append(named)
    chosen = dot_last(jnp.concatenate(chosen, axis=0), mine).astype(jnp.bfloat16)
    for j in range(chips):
        span = slice(j * chip_cols, (j + 1) * chip_cols)
        piece = jnp.dot(chosen, hid_all[j], preferred_element_type=jnp.float32)
        hid_ref[:, span] = piece[:rows].astype(jnp.bfloat16)
        part_send[:, span] = piece[rows:].astype(jnp.bfloat16)
    part_copy = remote(part_send, part_recv, psend_sem, precv_sem, sibling)
    part_copy.start()

    to_base = dot_last(owned, control_row(tokens, 0)).astype(jnp.bfloat16)

    def attend(queries, keys, values):
        queries = jnp.dot(to_base, queries, preferred_element_type=jnp.float32).astype(jnp.bfloat16)
        scores = dot_last(queries, keys) / math.sqrt(HEAD_DIM)
        expo = jnp.exp(scores - jnp.max(scores, axis=1, keepdims=True))
        denom = jnp.sum(expo, axis=1, keepdims=True)
        summed = jnp.dot(expo.astype(jnp.bfloat16), values, preferred_element_type=jnp.float32)
        out_send[...] = summed / denom

    head = line * 3 + row + core

    @pl.when(takes_own)
    def _():
        remote(
            qkv_own.at[1 - core], qkv_own.at[1 - core], msend_sem.at[0], orecv_sem, sibling
        ).wait_recv()
        joined = jnp.concatenate([qkv_own[0], qkv_own[1]], axis=0)
        attend(*[joined[:, i * HEAD_DIM : (i + 1) * HEAD_DIM] for i in range(3)])

    @pl.when(takes_middle)
    def _():
        for at in ((0, 0), (1, 0), (1, 1)):
            remote(
                qkv_mid.at[at[0], at[1]],
                qkv_mid.at[at[0], at[1]],
                msend_sem.at[1],
                mrecv_sem.at[at[0] * 2 + at[1]],
                sibling,
            ).wait_recv()
        joined = jnp.concatenate(
            [qkv_mid[0, which] + qkv_mid[1, which] for which in range(2)], axis=0
        )
        attend(*[joined[:, i * HEAD_DIM : (i + 1) * HEAD_DIM] for i in range(3)])

    works = jnp.logical_or(takes_own, takes_middle)

    def out_copy(step):
        target = lax.rem(me + step, seq)
        return remote(
            out_send.at[pl.ds(pl.multiple_of(target * rows, rows), rows)],
            out_recv.at[head],
            asend_sem.at[step],
            arecv_sem.at[head],
            target,
        )

    @pl.when(works)
    def _():
        for step in range(1, seq):
            out_copy(step).start()
        out_recv[head] = out_send[pl.ds(pl.multiple_of(me * rows, rows), rows), :]

    part_copy.wait_recv()
    hid_ref[...] = hid_ref[...] + part_recv[...]

    for copy in cond_copies + base_copies + weight_copies + hid_copies:
        copy.wait_send()

    @pl.when(jnp.logical_not(takes_own))
    def _():
        own_copy.wait_send()

    @pl.when(jnp.logical_not(takes_middle))
    def _():
        mid_copy.wait_send()

    part_copy.wait_send()

    for h in range(heads):
        which = h % 3
        source = (h // 3) * 4 + (0, 1, 3)[which]

        @pl.when(source != me)
        def _():
            remote(
                out_recv.at[h], out_recv.at[h], asend_sem.at[0], arecv_sem.at[h], sibling
            ).wait_recv()

        att_ref[:, h * HEAD_DIM : (h + 1) * HEAD_DIM] = out_recv[h].astype(jnp.bfloat16)

    @pl.when(works)
    def _():
        for step in range(1, seq):
            out_copy(step).wait_send()


def on_device_fused(
    seq,
    control, mask_ids, owner, mask_table, res_weight, base, modulation, q_weight, k_weight, v_weight
):
    rows, width = control.shape
    chips = seq // 2
    heads_width = q_weight.shape[1] * seq
    fits = (
        seq % 4 == 0
        and rows == 8
        and width % (chips * HEAD_DIM) == 0
        and q_weight.shape[1] * 8 == 3 * 2 * HEAD_DIM
        and (rows * seq) % HEAD_DIM == 0
        and rows * seq <= 256
    )
    if not fits:
        return on_device(
            control, mask_ids, owner, mask_table, res_weight, base, modulation, q_weight, k_weight, v_weight
        )
    tokens = rows * seq
    half = tokens // 2
    chip_cols = width // chips
    bf16 = jnp.bfloat16
    vmem = pl.BlockSpec(memory_space=pltpu.VMEM)
    hbm = pl.BlockSpec(memory_space=pl.ANY)
    dma = pltpu.SemaphoreType.DMA
    lines = chips // 2
    return pl.pallas_call(
        functools.partial(fused_kernel, seq),
        out_shape=(
            jax.ShapeDtypeStruct((rows, width), bf16),
            jax.ShapeDtypeStruct((rows, heads_width), bf16),
        ),
        in_specs=[vmem, pl.BlockSpec(memory_space=pltpu.SMEM)] + [hbm] * 8,
        out_specs=(vmem, vmem),
        scratch_shapes=[
            pltpu.VMEM(mask_table.shape, bf16),
            pltpu.VMEM(modulation.shape, jnp.float32),
            pltpu.VMEM((rows, width), bf16),
            pltpu.VMEM((rows, width), bf16),
            pltpu.VMEM((2, res_weight.shape[1], width), bf16),
            pltpu.VMEM((3, 2, q_weight.shape[1], width), bf16),
            pltpu.VMEM((chips, rows, width), bf16),
            pltpu.VMEM((seq, chips, rows, chip_cols), bf16),
            pltpu.VMEM((chips, half, chip_cols), bf16),
            pltpu.VMEM((2, half, 3 * HEAD_DIM), bf16),
            pltpu.VMEM((2, 2, half, 3 * HEAD_DIM), bf16),
            pltpu.VMEM((rows, width), bf16),
            pltpu.VMEM((rows, width), bf16),
            pltpu.VMEM((tokens, HEAD_DIM), jnp.float32),
            pltpu.VMEM((heads_width // HEAD_DIM, rows, HEAD_DIM), jnp.float32),
            dma((8,)),
            dma((4,)),
            dma((4,)),
            dma((2 * lines,)),
            dma((chips,)),
            dma((seq,)),
            dma((seq,)),
            dma((2 * lines,)),
            dma((chips,)),
            dma((2,)),
            dma(()),
            dma((4,)),
            dma(()),
            dma(()),
            dma((seq,)),
            dma((heads_width // HEAD_DIM,)),
        ],
        compiler_params=pltpu.CompilerParams(
            collective_id=0, has_side_effects=True, vmem_limit_bytes=56 * 1024 * 1024
        ),
    )(
        owner.reshape(1, tokens),
        mask_ids,
        mask_table,
        modulation,
        control,
        base,
        res_weight.T,
        q_weight.T,
        k_weight.T,
        v_weight.T,
    )


def solution(mesh):
    in_specs = (
        P(("parts", "seq"), None),
        P(("parts", "seq")),
        P("parts"),
        P(),
        P(None, "seq"),
        P(("parts", "seq"), None),
        P(),
        P(None, "seq"),
        P(None, "seq"),
        P(None, "seq"),
    )
    out_specs = (P(("parts", "seq"), None), P(("parts", "seq"), None))
    body = functools.partial(on_device_fused, mesh.shape["seq"])
    return jax.shard_map(
        body, mesh=mesh, in_specs=in_specs, out_specs=out_specs, check_vma=False
    )
```

```python
import functools
import math

import jax
import jax.numpy as jnp
from jax import lax
from jax.experimental import pallas as pl
from jax.experimental.pallas import tpu as pltpu
from jax.sharding import PartitionSpec as P

HEADS = 12
HEAD_DIM = 128


def layer_norm(hidden, modulation):
    row_mean = jnp.mean(hidden, axis=1, keepdims=True)
    centred = hidden - row_mean
    row_var = jnp.mean(centred * centred, axis=1, keepdims=True)
    scaled = centred * lax.rsqrt(row_var + 1e-06)
    return (scaled * (1.0 + modulation[1]) + modulation[0]).astype(jnp.bfloat16)


def attend_block(carried, segments, query_heads):
    running_max, running_sum, summed = carried
    key_rows, values = segments
    block_rows = key_rows.shape[0]
    key_heads = key_rows.reshape(block_rows, HEADS, HEAD_DIM)
    value_heads = values.reshape(block_rows, HEADS, HEAD_DIM)
    scores = jnp.einsum(
        "thd,khd->thk", query_heads, key_heads, preferred_element_type=jnp.float32
    ) / math.sqrt(HEAD_DIM)
    new_max = jnp.maximum(running_max, jnp.max(scores, axis=2))
    weights = jnp.exp(scores - new_max[:, :, None])
    running_sum = jnp.sum(weights, axis=2)
    summed = jnp.einsum(
        "thk,khd->thd",
        weights.astype(jnp.bfloat16),
        value_heads,
        preferred_element_type=jnp.float32,
    )
    return (new_max, running_sum, summed)


def on_device(
    control, mask_ids, owner, mask_table, res_weight, base, modulation, q_weight, k_weight, v_weight
):
    row_count = base.shape[0]
    selector = (
        mask_ids[:, None] == jnp.arange(mask_table.shape[0], dtype=jnp.int32)[None, :]
    ).astype(jnp.bfloat16)
    condition = (
        control.astype(jnp.float32)
        + jnp.dot(selector, mask_table, preferred_element_type=jnp.float32)
    ).astype(jnp.bfloat16)
    residual = jnp.dot(
        lax.all_gather(condition, "seq", axis=0, tiled=True),
        res_weight,
        preferred_element_type=jnp.float32,
    ).astype(jnp.bfloat16)
    total_rows = owner.shape[0]
    inverse = (
        jnp.zeros((total_rows,), jnp.int32).at[owner].set(jnp.arange(total_rows, dtype=jnp.int32))
    )
    relayed = lax.all_to_all(
        jnp.take(residual, inverse, axis=0), "seq", split_axis=0, concat_axis=1, tiled=True
    )
    hidden = base.astype(jnp.float32) + relayed.astype(jnp.float32)
    normed = layer_norm(hidden, modulation)
    joined = jnp.concatenate([q_weight, k_weight, v_weight], axis=1)
    col_width = q_weight.shape[1]
    columns = jnp.dot(
        lax.all_gather(normed, "seq", axis=0, tiled=True),
        joined,
        preferred_element_type=jnp.float32,
    ).astype(jnp.bfloat16)
    q_cols = columns[:, :col_width]
    k_cols = columns[:, col_width : 2 * col_width]
    v_cols = columns[:, 2 * col_width :]
    initial = (
        jnp.full((row_count, HEADS), -1e30, jnp.float32),
        jnp.zeros((row_count, HEADS), jnp.float32),
        jnp.zeros((row_count, HEADS, HEAD_DIM), jnp.float32),
    )
    queries = lax.all_to_all(q_cols, "seq", split_axis=0, concat_axis=1, tiled=True)
    key_rows, values = (
        lax.all_gather(k_cols, "seq", axis=1, tiled=True),
        lax.all_gather(v_cols, "seq", axis=1, tiled=True),
    )
    query_heads = queries.reshape(row_count, HEADS, HEAD_DIM)
    running_max, running_sum, summed = attend_block(initial, (key_rows, values), query_heads)
    attended = (
        (summed / running_sum[:, :, None]).reshape(row_count, HEADS * HEAD_DIM).astype(jnp.bfloat16)
    )
    return (hidden.astype(jnp.bfloat16), attended)


def remote(src, dst, send_sem, recv_sem, target):
    return pltpu.make_async_remote_copy(
        src_ref=src,
        dst_ref=dst,
        send_sem=send_sem,
        recv_sem=recv_sem,
        device_id={"seq": target},
        device_id_type=pl.DeviceIdType.MESH,
    )


def dot_last(a, b):
    return lax.dot_general(
        a, b, (((1,), (1,)), ((), ())), preferred_element_type=jnp.float32
    )


def one_hot(condition):
    return jnp.where(condition, 1.0, 0.0).astype(jnp.bfloat16)


def fused_kernel(
    seq,
    owner_ref,
    ids_ref,
    table_hbm,
    mod_hbm,
    control_hbm,
    base_hbm,
    wres_hbm,
    wq_hbm,
    wk_hbm,
    wv_hbm,
    hid_ref,
    att_ref,
    table_ref,
    mod_ref,
    control_ref,
    base_ref,
    wres,
    wqkv,
    cond_all,
    base_all,
    hid_all,
    qkv_own,
    qkv_mid,
    part_send,
    part_recv,
    out_send,
    out_recv,
    load_sem,
    wsend_sem,
    wrecv_sem,
    csend_sem,
    crecv_sem,
    bsend_sem,
    brecv_sem,
    hsend_sem,
    hrecv_sem,
    msend_sem,
    orecv_sem,
    mrecv_sem,
    psend_sem,
    precv_sem,
    asend_sem,
    arecv_sem,
):
    me = lax.axis_index("seq")
    core = lax.rem(me, 2)
    chip = lax.div(me, 2)
    row = lax.rem(chip, 2)
    line = lax.div(chip, 2)
    chips = seq // 2
    lines = chips // 2
    sibling = chip * 2 + 1 - core
    rows, width = control_hbm.shape
    tokens = rows * seq
    half = tokens // 2
    chip_cols = width // chips
    heads = att_ref.shape[1] // HEAD_DIM

    weights = (wres_hbm, wq_hbm, wk_hbm, wv_hbm)

    def slot(i, which):
        return wres.at[which] if i == 0 else wqkv.at[i - 1, which]

    loads = [
        pltpu.make_async_copy(weights[i], slot(i, core), load_sem.at[i]) for i in range(4)
    ]
    inputs = (
        (control_hbm, control_ref),
        (table_hbm, table_ref),
        (base_hbm, base_ref),
        (mod_hbm, mod_ref),
    )
    for i, (source, kept) in enumerate(inputs):
        loads.append(pltpu.make_async_copy(source, kept, load_sem.at[4 + i]))
    for load in loads[4:] + loads[:4]:
        load.start()

    barrier = pltpu.get_barrier_semaphore()
    for step in range(1, seq):
        pl.semaphore_signal(
            barrier,
            inc=1,
            device_id={"seq": lax.rem(me + step, seq)},
            device_id_type=pl.DeviceIdType.MESH,
        )

    for load in loads[4:]:
        load.wait()
    row_at = lax.broadcasted_iota(jnp.int32, (rows, width), 0)
    kinds = jnp.zeros((rows, width), jnp.int32)
    for r in range(rows):
        kinds = jnp.where(row_at == r, ids_ref[r], kinds)
    picked = jnp.zeros((rows, width), jnp.float32)
    for kind in range(table_ref.shape[0]):
        entry = table_ref[kind : kind + 1, :].astype(jnp.float32)
        picked = jnp.where(kinds == kind, entry, picked)
    cond_all[chip] = (control_ref[...].astype(jnp.float32) + picked).astype(jnp.bfloat16)
    for j in range(chips):
        base_all[me, j] = base_ref[:, j * chip_cols : (j + 1) * chip_cols]

    pl.semaphore_wait(barrier, seq - 1)

    def along(step):
        return lax.rem(line + step, lines) * 2

    def gather_sends(buf, send_sem, recv_sem):
        copies = []
        for step in range(1, lines):
            target = (along(step) + row) * 2 + core
            copies.append(
                remote(buf.at[chip], buf.at[chip], send_sem.at[step], recv_sem.at[chip], target)
            )
        target = (line * 2 + 1 - row) * 2 + core
        copies.insert(
            0, remote(buf.at[chip], buf.at[chip], send_sem.at[0], recv_sem.at[chip], target)
        )
        for copy in copies:
            copy.start()
        return copies

    across = (line * 2 + 1 - row) * 2 + core

    def arrival(buf, send_sem, recv_sem, source):
        remote(buf.at[source], buf.at[source], send_sem.at[0], recv_sem.at[source], across).wait_recv()

    def forward(buf, send_sem, recv_sem, step):
        source = along(lines - step) + row
        arrival(buf, send_sem, recv_sem, source)
        copy = remote(
            buf.at[source], buf.at[source], send_sem.at[lines - 1 + step], recv_sem.at[source], across
        )
        copy.start()
        return source, copy

    cond_copies = gather_sends(cond_all, csend_sem, crecv_sem)
    weight_copies = [
        remote(weights[i], slot(i, core), wsend_sem.at[i], wrecv_sem.at[i], sibling)
        for i in range(4)
    ]
    weight_copies[0].start()

    base_copies = []
    for step in range(1, seq):
        target = lax.rem(me + step, seq)
        copy = remote(
            base_all.at[me, lax.div(target, 2)],
            base_all.at[me, lax.div(target, 2)],
            bsend_sem.at[step],
            brecv_sem.at[me],
            target,
        )
        copy.start()
        base_copies.append(copy)
    for copy in weight_copies[1:]:
        copy.start()

    for step in range(1, lines):
        cond_copies.append(forward(cond_all, csend_sem, crecv_sem, step)[1])

    owned = one_hot(
        lax.broadcasted_iota(jnp.int32, (tokens, tokens), 0) == owner_ref[...]
    )

    def control_row(count, first):
        at = first + lax.broadcasted_iota(jnp.int32, (count, tokens), 0)
        part = jnp.where(at >= half, 1, 0)
        inner = at - part * half
        shift = rows.bit_length() - 1
        index = (
            lax.shift_left(lax.shift_right_logical(inner, shift), shift + 1)
            + part * rows
            + lax.bitwise_and(inner, rows - 1)
        )
        return one_hot(index == lax.broadcasted_iota(jnp.int32, (count, tokens), 1))

    mine = control_row(half, core * half)
    base_of = dot_last(mine, owned).astype(jnp.bfloat16)

    loads[0].wait()
    weight_copies[0].wait_recv()
    arrival(cond_all, csend_sem, crecv_sem, across // 2)
    for step in range(1, lines):
        arrival(cond_all, csend_sem, crecv_sem, along(lines - step) + 1 - row)
    for step in range(1, seq):
        source = lax.rem(me + seq - step, seq)
        remote(
            base_all.at[source, chip],
            base_all.at[source, chip],
            bsend_sem.at[step],
            brecv_sem.at[source],
            sibling,
        ).wait_recv()

    condition = cond_all[...].reshape(half, width)
    residual = dot_last(condition, wres[...].reshape(chip_cols, width)).astype(jnp.bfloat16)
    base_cols = jnp.concatenate([base_all[s, chip] for s in range(seq)], axis=0)
    base_rows = jnp.dot(base_of, base_cols, preferred_element_type=jnp.float32)
    hid_all[chip] = (base_rows + residual.astype(jnp.float32)).astype(jnp.bfloat16)

    hid_copies = gather_sends(hid_all, hsend_sem, hrecv_sem)

    for i in range(1, 4):
        loads[i].wait()
        weight_copies[i].wait_recv()

    local = 2 * wqkv.shape[2]
    row_of = lax.broadcasted_iota(jnp.int32, (rows, width), 0)
    affine = jnp.where(row_of == 0, 1.0 + mod_ref[1:2, :], jnp.where(row_of == 1, mod_ref[0:1, :], 0.0))
    coarse = affine.astype(jnp.bfloat16).astype(jnp.float32)
    affine = jnp.concatenate([coarse, affine - coarse], axis=0).astype(jnp.bfloat16)
    affine = [dot_last(affine, wqkv[i].reshape(local, width)) for i in range(3)]
    affine = [both[:rows] + both[rows:] for both in affine]
    sums = [jnp.zeros((half, 1), jnp.float32)]
    columns = [jnp.zeros((half, local), jnp.float32) for _ in range(3)]

    def consume(j):
        span = pl.ds(pl.multiple_of(j * chip_cols, HEAD_DIM), chip_cols)
        block = hid_all[j].astype(jnp.float32)
        sums[0] += jnp.sum(block, axis=1, keepdims=True)
        gained = (block * (1.0 + mod_ref[1:2, span])).astype(jnp.bfloat16)
        for i in range(3):
            columns[i] += dot_last(gained, wqkv[i, :, :, span].reshape(local, chip_cols))

    consume(chip)
    for step in range(1, lines):
        source, copy = forward(hid_all, hsend_sem, hrecv_sem, step)
        hid_copies.append(copy)
        if step == 1:
            arrival(hid_all, hsend_sem, hrecv_sem, across // 2)
            consume(across // 2)
        consume(source)
    for step in range(1, lines):
        source = along(lines - step) + 1 - row
        arrival(hid_all, hsend_sem, hrecv_sem, source)
        consume(source)

    mean = sums[0] / width
    total = jnp.zeros((half, 1), jnp.float32)
    for j in range(chips):
        centred = hid_all[j].astype(jnp.float32) - mean
        total += jnp.sum(centred * centred, axis=1, keepdims=True)
    scale = lax.rsqrt(total / width + 1e-06)
    columns = [
        (columns[i] - mean * affine[i][0:1]) * scale + affine[i][1:2] for i in range(3)
    ]

    blank = jnp.zeros((half, 2 * HEAD_DIM - local), jnp.float32)
    for i in range(3):
        first = jnp.concatenate([columns[i], blank], axis=1)
        second = jnp.concatenate([blank, columns[i]], axis=1)
        own = jnp.where(row == 0, first[:, :HEAD_DIM], second[:, HEAD_DIM:])
        middle = jnp.where(row == 0, first[:, HEAD_DIM:], second[:, :HEAD_DIM])
        span = slice(i * HEAD_DIM, (i + 1) * HEAD_DIM)
        qkv_own[core, :, span] = own.astype(jnp.bfloat16)
        qkv_mid[row, core, :, span] = middle.astype(jnp.bfloat16)

    middle_at = line * 4 + 1
    takes_own = core == row
    takes_middle = jnp.logical_and(row == 0, core == 1)
    own_copy = remote(
        qkv_own.at[core], qkv_own.at[core], msend_sem.at[0], orecv_sem, sibling
    )
    mid_copy = remote(
        qkv_mid.at[row, core],
        qkv_mid.at[row, core],
        msend_sem.at[1],
        mrecv_sem.at[row * 2 + core],
        middle_at,
    )

    @pl.when(jnp.logical_not(takes_own))
    def _():
        own_copy.start()

    @pl.when(jnp.logical_not(takes_middle))
    def _():
        mid_copy.start()

    chosen = []
    for first in (me * rows, sibling * rows):
        named = one_hot(
            first + lax.broadcasted_iota(jnp.int32, (rows, tokens), 0) == owner_ref[...]
        )
        chosen.append(named)
    chosen = dot_last(jnp.concatenate(chosen, axis=0), mine).astype(jnp.bfloat16)
    for j in range(chips):
        span = slice(j * chip_cols, (j + 1) * chip_cols)
        piece = jnp.dot(chosen, hid_all[j], preferred_element_type=jnp.float32)
        hid_ref[:, span] = piece[:rows].astype(jnp.bfloat16)
        part_send[:, span] = piece[rows:].astype(jnp.bfloat16)
    part_copy = remote(part_send, part_recv, psend_sem, precv_sem, sibling)
    part_copy.start()

    to_base = dot_last(owned, control_row(tokens, 0)).astype(jnp.bfloat16)

    def attend(queries, keys, values):
        queries = jnp.dot(to_base, queries, preferred_element_type=jnp.float32).astype(jnp.bfloat16)
        scores = dot_last(queries, keys) / math.sqrt(HEAD_DIM)
        expo = jnp.exp(scores - jnp.max(scores, axis=1, keepdims=True))
        denom = jnp.sum(expo, axis=1, keepdims=True)
        summed = jnp.dot(expo.astype(jnp.bfloat16), values, preferred_element_type=jnp.float32)
        out_send[...] = summed / denom

    head = line * 3 + row + core

    @pl.when(takes_own)
    def _():
        remote(
            qkv_own.at[1 - core], qkv_own.at[1 - core], msend_sem.at[0], orecv_sem, sibling
        ).wait_recv()
        joined = jnp.concatenate([qkv_own[0], qkv_own[1]], axis=0)
        attend(*[joined[:, i * HEAD_DIM : (i + 1) * HEAD_DIM] for i in range(3)])

    @pl.when(takes_middle)
    def _():
        for at in ((0, 0), (1, 0), (1, 1)):
            remote(
                qkv_mid.at[at[0], at[1]],
                qkv_mid.at[at[0], at[1]],
                msend_sem.at[1],
                mrecv_sem.at[at[0] * 2 + at[1]],
                sibling,
            ).wait_recv()
        joined = jnp.concatenate(
            [qkv_mid[0, which] + qkv_mid[1, which] for which in range(2)], axis=0
        )
        attend(*[joined[:, i * HEAD_DIM : (i + 1) * HEAD_DIM] for i in range(3)])

    works = jnp.logical_or(takes_own, takes_middle)

    def out_copy(step):
        target = lax.rem(me + step, seq)
        return remote(
            out_send.at[pl.ds(pl.multiple_of(target * rows, rows), rows)],
            out_recv.at[head],
            asend_sem.at[step],
            arecv_sem.at[head],
            target,
        )

    @pl.when(works)
    def _():
        for step in range(1, seq):
            out_copy(step).start()
        out_recv[head] = out_send[pl.ds(pl.multiple_of(me * rows, rows), rows), :]

    part_copy.wait_recv()
    hid_ref[...] = hid_ref[...] + part_recv[...]

    for copy in cond_copies + base_copies + weight_copies + hid_copies:
        copy.wait_send()

    @pl.when(jnp.logical_not(takes_own))
    def _():
        own_copy.wait_send()

    @pl.when(jnp.logical_not(takes_middle))
    def _():
        mid_copy.wait_send()

    part_copy.wait_send()

    for h in range(heads):
        which = h % 3
        source = (h // 3) * 4 + (0, 1, 3)[which]

        @pl.when(source != me)
        def _():
            remote(
                out_recv.at[h], out_recv.at[h], asend_sem.at[0], arecv_sem.at[h], sibling
            ).wait_recv()

        att_ref[:, h * HEAD_DIM : (h + 1) * HEAD_DIM] = out_recv[h].astype(jnp.bfloat16)

    @pl.when(works)
    def _():
        for step in range(1, seq):
            out_copy(step).wait_send()


def on_device_fused(
    seq,
    control, mask_ids, owner, mask_table, res_weight, base, modulation, q_weight, k_weight, v_weight
):
    rows, width = control.shape
    chips = seq // 2
    heads_width = q_weight.shape[1] * seq
    fits = (
        seq % 4 == 0
        and rows == 8
        and width % (chips * HEAD_DIM) == 0
        and q_weight.shape[1] * 8 == 3 * 2 * HEAD_DIM
        and (rows * seq) % HEAD_DIM == 0
        and rows * seq <= 256
    )
    if not fits:
        return on_device(
            control, mask_ids, owner, mask_table, res_weight, base, modulation, q_weight, k_weight, v_weight
        )
    tokens = rows * seq
    half = tokens // 2
    chip_cols = width // chips
    bf16 = jnp.bfloat16
    vmem = pl.BlockSpec(memory_space=pltpu.VMEM)
    hbm = pl.BlockSpec(memory_space=pl.ANY)
    dma = pltpu.SemaphoreType.DMA
    lines = chips // 2
    return pl.pallas_call(
        functools.partial(fused_kernel, seq),
        out_shape=(
            jax.ShapeDtypeStruct((rows, width), bf16),
            jax.ShapeDtypeStruct((rows, heads_width), bf16),
        ),
        in_specs=[vmem, pl.BlockSpec(memory_space=pltpu.SMEM)] + [hbm] * 8,
        out_specs=(vmem, vmem),
        scratch_shapes=[
            pltpu.VMEM(mask_table.shape, bf16),
            pltpu.VMEM(modulation.shape, jnp.float32),
            pltpu.VMEM((rows, width), bf16),
            pltpu.VMEM((rows, width), bf16),
            pltpu.VMEM((2, res_weight.shape[1], width), bf16),
            pltpu.VMEM((3, 2, q_weight.shape[1], width), bf16),
            pltpu.VMEM((chips, rows, width), bf16),
            pltpu.VMEM((seq, chips, rows, chip_cols), bf16),
            pltpu.VMEM((chips, half, chip_cols), bf16),
            pltpu.VMEM((2, half, 3 * HEAD_DIM), bf16),
            pltpu.VMEM((2, 2, half, 3 * HEAD_DIM), bf16),
            pltpu.VMEM((rows, width), bf16),
            pltpu.VMEM((rows, width), bf16),
            pltpu.VMEM((tokens, HEAD_DIM), jnp.float32),
            pltpu.VMEM((heads_width // HEAD_DIM, rows, HEAD_DIM), jnp.float32),
            dma((8,)),
            dma((4,)),
            dma((4,)),
            dma((2 * lines,)),
            dma((chips,)),
            dma((seq,)),
            dma((seq,)),
            dma((2 * lines,)),
            dma((chips,)),
            dma((2,)),
            dma(()),
            dma((4,)),
            dma(()),
            dma(()),
            dma((seq,)),
            dma((heads_width // HEAD_DIM,)),
        ],
        compiler_params=pltpu.CompilerParams(
            collective_id=0, has_side_effects=True, vmem_limit_bytes=56 * 1024 * 1024
        ),
    )(
        owner.reshape(1, tokens),
        mask_ids,
        mask_table,
        modulation,
        control,
        base,
        res_weight.T,
        q_weight.T,
        k_weight.T,
        v_weight.T,
    )


def solution(mesh):
    in_specs = (
        P(("parts", "seq"), None),
        P(("parts", "seq")),
        P("parts"),
        P(),
        P(None, "seq"),
        P(("parts", "seq"), None),
        P(),
        P(None, "seq"),
        P(None, "seq"),
        P(None, "seq"),
    )
    out_specs = (P(("parts", "seq"), None), P(("parts", "seq"), None))
    body = functools.partial(on_device_fused, mesh.shape["seq"])
    return jax.shard_map(
        body, mesh=mesh, in_specs=in_specs, out_specs=out_specs, check_vma=False
    )
```
